32 devices in a mesh: expert: 16 (over z, y, core), dp: 2 (over x).
Axes of the slice: x: 2, y: 2, z: 4, core: 2. Of those that a mesh axis runs over, the one named last changes fastest.
Arguments:
- tokens: bfloat16 [16, 7168], P('dp', 'expert'), may hold values from -6 to 6
- expert_ids: int32 [16, 8], P('dp'), may hold values from 0 to 15, all different within a row; in each aligned block of 8 rows (0 to 7, 8 to 15, ...) at most 8 rows name the same one
- gate_values: float32 [16, 8], P('dp'), may hold values from 0.05 to 1
- w_gate: bfloat16 [16, 2048, 7168], P('expert', 'dp'), may hold values from -0.0625 to 0.0625
- w_up: bfloat16 [16, 2048, 7168], P('expert', 'dp'), may hold values from -0.0625 to 0.0625
- w_down: bfloat16 [16, 2048, 7168], P('expert', 'dp'), may hold values from -0.125 to 0.125
Outputs:
- mixed: bfloat16 [16, 7168], P('dp', 'expert')
The draws below stay inside these ranges and needn't reach their ends.
Inputs may be any that keep to these rules, and one draw needn't show every extreme that they name: `expert_ids`: each token names 8 different experts; among the 8 tokens of one index of dp no expert is named more than 8 times, and in every draw some expert is named exactly 8 times by one such block.
All inputs are finite; a program needn't handle non-finite values.
Results may differ from the reference program's by a relative error of at most 0.0051.
Values may be sent and summed in bfloat16 or wider, within the bound.
A program may use at most 192 MiB of HBM per device.

```python
import math
import jax
import jax.numpy as jnp
import numpy as np
from jax import lax

D = 7168
FF = 2048
TOP = 8
TOK_DEV = 8
EXPERTS = 16
CAP = 8
TOKENS = 16
N_DP = 2


def levels(key, extent, cuts, least, largest):
    level = 1.0
    for axis_at, shards_of in cuts:
        steps = jax.random.uniform(jax.random.fold_in(jax.random.fold_in(key, 6), axis_at), (shards_of,), jnp.float32, least / len(cuts), largest / len(cuts))
        level = level * jnp.repeat(jnp.exp(steps), extent[axis_at] // shards_of).reshape((-1,) + (1,) * (len(extent) - 1 - axis_at))
    return level


def assign_block(rng, own, number, rows, number_of, top, limit, skew):
    order = jax.random.permutation(rng, number_of)
    crowded, ordinary = load_shares(number_of, rows * top, limit, skew, True), load_shares(number_of, rows * top, limit, skew, False)
    places = jnp.arange(number_of)

    def named(tallies, offset_by):
        used = int((tallies > 0).sum())
        fixed = max(1, used // 4)
        moved = fixed + (places - fixed + offset_by * (used - fixed)) % max(1, number_of - fixed)
        return jnp.zeros((number_of,), jnp.int32).at[order[jnp.where(places < fixed, places, moved)]].set(jnp.asarray(tallies, jnp.int32))

    tallies = jnp.where(number % 4 == 0, named(crowded, number // 4), named(ordinary, number - number // 4 - 1))
    mixed = jax.random.permutation(jax.random.fold_in(own, 3), number_of)
    giver, taker = mixed[0:number_of // 2 * 2:2], mixed[1:number_of // 2 * 2:2]
    room = jnp.minimum(tallies[giver] - 1, limit - tallies[taker]) // 2
    room = jnp.where((giver == order[0]) | (taker == order[0]) | (tallies[taker] == 0), 0, jnp.maximum(room, 0))
    moved = jax.random.randint(jax.random.fold_in(own, 4), (number_of // 2,), 0, 1 << 20) % (room + 1)
    tallies = tallies.at[giver].add(-moved).at[taker].add(moved)
    items = jnp.searchsorted(jnp.cumsum(tallies), jnp.arange(rows * top), side="right").astype(jnp.int32)
    grid = items.reshape(top, rows).T
    grid = grid[jax.random.permutation(jax.random.fold_in(own, 1), rows)]
    offset_by = jax.random.randint(jax.random.fold_in(own, 2), (rows, 1), 0, top)
    return jnp.take_along_axis(grid, (jnp.arange(top)[None, :] + offset_by) % top, axis=1)


def load_shares(number_of, total, limit, slope, full):
    loads = [(1 << 20) // math.isqrt(grade ** slope) + 1 for grade in range(1, number_of + 1)]
    largest = limit if full else min(limit, max(-(-total // number_of), total * loads[0] // sum(loads)))
    least = 1 if total - largest >= number_of - 1 else 0
    counts, spare = [largest] + [least] * (number_of - 1), total - largest - least * (number_of - 1)
    while spare > 0:
        movable = [i for i in range(1, number_of) if counts[i] < largest] or [i for i in range(1, number_of) if counts[i] < limit]
        pool, remaining = sum([loads[i] for i in movable]), spare
        for i in movable:
            extra = min(limit - counts[i], max(1, remaining * loads[i] // pool), spare)
            counts[i] = counts[i] + extra
            spare = spare - extra
    return np.array(counts)


def gaussian(own_key, dims, spread, reach, cuts=(), kind=jnp.bfloat16):
    result = jax.random.normal(own_key, dims, jnp.float32) * spread
    if len(cuts) > 0:
        result = levels(own_key, dims, cuts, -0.22, 0.18) * result
    return jnp.clip(result, min=-reach, max=reach).astype(kind)


def setup_inputs(seed: int = 0) -> dict:
    key_of = jax.random.split(jax.random.key(seed), 7)
    tokens = gaussian(key_of[0], (TOKENS, D), 1.0, 6.0, ((0, 2), (1, 16)))
    expert_ids_keys = jax.random.split(jax.random.fold_in(key_of[1], 1), TOKENS // TOK_DEV)
    expert_ids_turns = jax.random.permutation(jax.random.fold_in(key_of[1], 3), TOKENS // TOK_DEV)
    expert_ids = jax.vmap(lambda own, number: assign_block(jax.random.fold_in(key_of[1], 2), own, number, TOK_DEV, EXPERTS, TOP, CAP, 2))(expert_ids_keys, expert_ids_turns).reshape((TOKENS, TOP))
    gate_values = jnp.clip(jnp.exp(math.log(1.0) - 2.9957323 * jax.random.uniform(key_of[2], (TOKENS, TOP), jnp.float32) ** levels(key_of[2], (TOKENS, TOP), ((0, 2),), -0.2, 0.2)), 0.05, 1.0)
    w_gate = gaussian(key_of[3], (EXPERTS, FF, D), D ** -0.5, 0.0625, ((0, 16), (1, 2)))
    w_up = gaussian(key_of[4], (EXPERTS, FF, D), D ** -0.5, 0.0625, ((0, 16), (1, 2)))
    w_down = gaussian(key_of[5], (EXPERTS, FF, D), FF ** -0.5, 0.125, ((0, 16), (1, 2)))
    return {"tokens": tokens, "expert_ids": expert_ids, "gate_values": gate_values, "w_gate": w_gate, "w_up": w_up, "w_down": w_down}


def slot_targets(expert_ids):
    flat = expert_ids.reshape(N_DP, TOK_DEV * TOP)
    onehot = (flat[..., None] == jnp.arange(EXPERTS, dtype=jnp.int32)).astype(jnp.int32)
    rank = jnp.cumsum(onehot, axis=1) - onehot
    slot = jnp.sum(rank * onehot, axis=-1)
    return (flat * CAP + slot).astype(jnp.int32)


def reference(tokens, expert_ids, gate_values, w_gate, w_up, w_down):
    target = slot_targets(expert_ids)
    blocks = tokens.reshape(N_DP, TOK_DEV, D).astype(jnp.float32)
    repeated = jnp.repeat(blocks, TOP, axis=1)

    def fill(pair):
        tgt, rep = pair
        place = (tgt[:, None] == jnp.arange(EXPERTS * CAP, dtype=jnp.int32)[None, :]).astype(jnp.float32)
        return jnp.dot(place.T, rep, preferred_element_type=jnp.float32).astype(jnp.bfloat16)

    buffer = lax.map(fill, (target, repeated))
    buffer = buffer.reshape(N_DP, EXPERTS, CAP, D).transpose(1, 0, 2, 3).reshape(EXPERTS, N_DP * CAP, D)

    def expert(pack):
        rows, wg, wu, wd = pack
        gate = jnp.dot(rows, wg.T, preferred_element_type=jnp.float32)
        upper = jnp.dot(rows, wu.T, preferred_element_type=jnp.float32)
        hidden = (jax.nn.silu(gate) * upper).astype(jnp.bfloat16)
        return jnp.dot(hidden, wd, preferred_element_type=jnp.float32)

    expert_out = lax.map(expert, (buffer, w_gate, w_up, w_down))
    per_block = expert_out.reshape(EXPERTS, N_DP, CAP, D).transpose(1, 0, 2, 3).reshape(N_DP, EXPERTS * CAP, D)
    picked = jnp.take_along_axis(per_block, target[..., None], axis=1)
    weights = gate_values.reshape(N_DP, TOK_DEV * TOP, 1)
    mixed = jnp.sum((picked * weights).reshape(N_DP, TOK_DEV, TOP, D), axis=2)
    return mixed.reshape(TOKENS, D).astype(jnp.bfloat16)
```

```python
import functools

import jax
import jax.numpy as jnp
from jax import lax
from jax.experimental import pallas as pl
from jax.experimental.pallas import tpu as pltpu
from jax.sharding import PartitionSpec as P

MESH = pl.DeviceIdType.MESH


def against_features(piece, weight):
    return lax.dot_general(
        piece, weight, (((1,), (1,)), ((), ())), preferred_element_type=jnp.float32
    )


def each(count, body):
    if count <= 4:
        for i in range(count):
            body(i)
    else:
        @pl.loop(0, count)
        def _(i):
            body(i)


def fold(block):
    half = block.shape[1] // 2
    return jnp.concatenate([block[:, :half], block[:, half:]], axis=0)


def unfold(block):
    half = block.shape[0] // 2
    return jnp.concatenate([block[:half], block[half:]], axis=1)


def kernel(
    n_exp, n_dp, hid_block, col_block,
    tok_ref, ids_ref, gates_ref, wg_hbm, wu_hbm, wd_hbm, out_ref,
    wg, wu, wd, stage, tokbuf, x, hid, y, sendbuf, recvbuf,
    g_sem, u_sem, d_sem, tok_send, tok_recv, out_send, out_recv,
):
    n_all = n_exp * n_dp
    rows, cols = tok_ref.shape
    n_hid = wg.shape[0]
    n_col = wd.shape[0]
    per = col_block // cols
    e_me = lax.axis_index("expert")
    d_me = lax.axis_index("dp")
    me = e_me * n_dp + d_me
    home = e_me // per

    def chunk_at(i):
        i = jnp.int32(i)
        turn = n_col // 2 + (1 - 2 * (i % 2)) * ((i + 1) // 2)
        return (home + turn) % n_col

    def copy_gate(i):
        at = pl.ds(i * hid_block, hid_block)
        return pltpu.make_async_copy(wg_hbm.at[at], wg.at[i], g_sem.at[i])

    def copy_up(i):
        at = pl.ds(i * hid_block, hid_block)
        return pltpu.make_async_copy(wu_hbm.at[at], wu.at[i], u_sem.at[i])

    def copy_down(i):
        start = pl.multiple_of(chunk_at(i) * col_block, 128)
        return pltpu.make_async_copy(
            wd_hbm.at[:, pl.ds(start, col_block)], wd.at[i], d_sem.at[i]
        )

    barrier = pltpu.get_barrier_semaphore()

    @pl.loop(1, n_all)
    def _(k):
        to = (me + k) % n_all
        pl.semaphore_signal(
            barrier, inc=1, device_id=(to // n_dp, to % n_dp), device_id_type=MESH
        )

    for i in range(n_hid):
        copy_gate(i).start()
        copy_up(i).start()
    for i in range(n_col):
        copy_down(i).start()

    stage[...] = fold(tok_ref[...].astype(jnp.float32)).astype(jnp.bfloat16)
    own = pltpu.make_async_copy(stage, tokbuf.at[me], tok_recv)
    own.start()
    pl.semaphore_wait(barrier, n_all - 1)

    @pl.loop(1, n_all)
    def _(k):
        to = (me + k) % n_all
        pltpu.make_async_remote_copy(
            src_ref=stage, dst_ref=tokbuf.at[me], send_sem=tok_send, recv_sem=tok_recv,
            device_id=(to // n_dp, to % n_dp), device_id_type=MESH,
        ).start()

    pltpu.make_async_copy(tokbuf, tokbuf, tok_recv).wait()

    def gather_rows(pair):
        halves = []
        for q in range(2):
            parts = [
                unfold(tokbuf[e * n_dp + pair * 2 + q].astype(jnp.float32))
                for e in range(n_exp)
            ]
            halves.append(jnp.concatenate(parts, axis=1))
        both = jnp.concatenate(halves, axis=0).astype(jnp.bfloat16)
        x[pl.ds(pair * 2 * rows, 2 * rows), :] = both

    each(n_dp // 2, gather_rows)

    @pl.loop(0, n_hid)
    def _(i):
        copy_gate(i).wait()
        gate = against_features(x[...], wg[i])
        copy_up(i).wait()
        upper = against_features(x[...], wu[i])
        hid[i] = (gate / (1.0 + jnp.exp(-gate)) * upper).astype(jnp.bfloat16)

    @pl.loop(0, n_col)
    def _(i):
        chunk = chunk_at(i)
        copy_down(i).wait()
        h = jnp.concatenate([hid[j] for j in range(n_hid)], axis=1)
        y[...] = jnp.dot(h, wd[i], preferred_element_type=jnp.float32)

        def send(d):
            for p in range(per):
                e_to = chunk * per + p
                to = e_to * n_dp + d
                block = y[pl.ds(d * rows, rows), p * cols:(p + 1) * cols]
                sendbuf[to] = fold(block).astype(jnp.bfloat16)

                @pl.when(to != me)
                def _():
                    pltpu.make_async_remote_copy(
                        src_ref=sendbuf.at[to], dst_ref=recvbuf.at[me],
                        send_sem=out_send, recv_sem=out_recv,
                        device_id=(e_to, d), device_id_type=MESH,
                    ).start()

                @pl.when(to == me)
                def _():
                    pltpu.make_async_copy(sendbuf.at[to], recvbuf.at[me], out_recv).start()

        each(n_dp, send)

    ids = ids_ref[...]
    gates = gates_ref[...]
    shares = []
    for e in range(n_exp):
        one = jnp.sum(jnp.where(ids == e, gates, 0.0), axis=1, keepdims=True)
        shares.append(jnp.concatenate([one, one], axis=0))
    pltpu.make_async_copy(recvbuf, recvbuf, out_recv).wait()
    total = jnp.zeros((2 * rows, cols // 2), jnp.float32)
    for e in range(n_exp):
        part = jnp.zeros((2 * rows, cols // 2), jnp.float32)
        for d in range(n_dp):
            part = part + recvbuf[e * n_dp + d].astype(jnp.float32)
        total = total + part * shares[e]
    out_ref[...] = unfold(total).astype(out_ref.dtype)

    pltpu.make_async_copy(
        tokbuf.at[pl.ds(0, n_all - 1)], tokbuf.at[pl.ds(0, n_all - 1)], tok_send
    ).wait()
    pltpu.make_async_copy(
        sendbuf.at[pl.ds(0, n_all - 1)], sendbuf.at[pl.ds(0, n_all - 1)], out_send
    ).wait()


def local(n_exp, n_dp, tokens, expert_ids, gate_values, w_gate, w_up, w_down):
    rows, cols = tokens.shape
    _, hidden, width = w_gate.shape
    all_rows = rows * n_dp
    n_all = n_exp * n_dp
    hid_block = min(256, hidden)
    col_block = cols
    while col_block % 128:
        col_block *= 2
    n_hid, n_col = hidden // hid_block, width // col_block
    vmem = pl.BlockSpec(memory_space=pltpu.VMEM)
    hbm = pl.BlockSpec(memory_space=pl.ANY)
    bf16, f32 = jnp.bfloat16, jnp.float32
    return pl.pallas_call(
        functools.partial(kernel, n_exp, n_dp, hid_block, col_block),
        out_shape=jax.ShapeDtypeStruct((rows, cols), bf16),
        in_specs=[vmem, vmem, vmem, hbm, hbm, hbm],
        out_specs=vmem,
        scratch_shapes=[
            pltpu.VMEM((n_hid, hid_block, width), bf16),
            pltpu.VMEM((n_hid, hid_block, width), bf16),
            pltpu.VMEM((n_col, hidden, col_block), bf16),
            pltpu.VMEM((2 * rows, cols // 2), bf16),
            pltpu.VMEM((n_all, 2 * rows, cols // 2), bf16),
            pltpu.VMEM((all_rows, width), bf16),
            pltpu.VMEM((n_hid, all_rows, hid_block), bf16),
            pltpu.VMEM((all_rows, col_block), f32),
            pltpu.VMEM((n_all, 2 * rows, cols // 2), bf16),
            pltpu.VMEM((n_all, 2 * rows, cols // 2), bf16),
            pltpu.SemaphoreType.DMA((n_hid,)),
            pltpu.SemaphoreType.DMA((n_hid,)),
            pltpu.SemaphoreType.DMA((n_col,)),
            pltpu.SemaphoreType.DMA,
            pltpu.SemaphoreType.DMA,
            pltpu.SemaphoreType.DMA,
            pltpu.SemaphoreType.DMA,
        ],
        compiler_params=pltpu.CompilerParams(
            collective_id=0, has_side_effects=True, vmem_limit_bytes=56 * 1024 * 1024
        ),
    )(tokens, expert_ids, gate_values, w_gate[0], w_up[0], w_down[0])


def solution(mesh):
    placed = (
        P("dp", "expert"),
        P("dp", None),
        P("dp", None),
        P("expert", "dp", None),
        P("expert", "dp", None),
        P("expert", "dp", None),
    )
    return jax.shard_map(
        functools.partial(local, mesh.shape["expert"], mesh.shape["dp"]),
        mesh=mesh, in_specs=placed, out_specs=P("dp", "expert"), check_vma=False,
    )
```

```python
import functools

import jax
import jax.numpy as jnp
from jax import lax
from jax.experimental import pallas as pl
from jax.experimental.pallas import tpu as pltpu
from jax.sharding import PartitionSpec as P

MESH = pl.DeviceIdType.MESH
AHEAD = 2
EARLY = 2


def against_features(piece, weight):
    return lax.dot_general(
        piece, weight, (((1,), (1,)), ((), ())), preferred_element_type=jnp.float32
    )


def spans(cols, col_block):
    first = [p * cols // 128 * 128 for p in range(col_block // cols)]
    need = max(p * cols - start + cols for p, start in enumerate(first))
    width = -(-need // 256) * 256
    return [min(start, col_block - width) for start in first], width


def each(count, body):
    if count <= 4:
        for i in range(count):
            body(i)
    else:
        @pl.loop(0, count)
        def _(i):
            body(i)


def fold(block):
    half = block.shape[1] // 2
    return jnp.concatenate([block[:, :half], block[:, half:]], axis=0)


def unfold(block):
    half = block.shape[0] // 2
    return jnp.concatenate([block[:half], block[half:]], axis=1)


def kernel(
    n_exp, n_dp, hid_block, col_block,
    tok_ref, ids_ref, gates_ref, wg_hbm, wu_hbm, wd_hbm, out_ref,
    wg, wu, wd, stage, tokbuf, x, hid, y, sendbuf, recvbuf,
    g_sem, u_sem, d_sem, tok_send, tok_recv, out_send, out_recv,
):
    n_all = n_exp * n_dp
    rows, cols = tok_ref.shape
    n_hid = wg.shape[0]
    n_col = wd.shape[0]
    per = col_block // cols
    n_pair = n_col // 2
    starts, span = spans(cols, col_block)
    early = min(EARLY, n_hid)
    e_me = lax.axis_index("expert")
    d_me = lax.axis_index("dp")
    me = e_me * n_dp + d_me
    home = e_me // per

    def chunk_at(i):
        i = jnp.int32(i)
        turn = n_col // 2 + (1 - 2 * (i % 2)) * ((i + 1) // 2)
        return (home + turn) % n_col

    def copy_gate(i):
        at = pl.ds(i * hid_block, hid_block)
        return pltpu.make_async_copy(wg_hbm.at[at], wg.at[i], g_sem.at[i])

    def copy_up(i):
        at = pl.ds(i * hid_block, hid_block)
        return pltpu.make_async_copy(wu_hbm.at[at], wu.at[i], u_sem.at[i])

    def copy_down(i):
        start = pl.multiple_of(chunk_at(i) * col_block, 128)
        return pltpu.make_async_copy(
            wd_hbm.at[:, pl.ds(start, col_block)], wd.at[i], d_sem.at[i]
        )

    barrier = pltpu.get_barrier_semaphore()

    @pl.loop(1, n_all)
    def _(k):
        to = (me + k) % n_all
        pl.semaphore_signal(
            barrier, inc=1, device_id=(to // n_dp, to % n_dp), device_id_type=MESH
        )

    def start_hid(i):
        copy_gate(i).start()
        copy_up(i).start()

    def start_step(i):
        if isinstance(i, int):
            if i < n_hid:
                start_hid(i)
            elif i < n_hid + n_pair:
                copy_down(2 * (i - n_hid)).start()
                copy_down(2 * (i - n_hid) + 1).start()
            return
        pl.when(i < n_hid)(lambda: start_hid(i))

        @pl.when((i >= n_hid) & (i < n_hid + n_pair))
        def _():
            copy_down(2 * (i - n_hid)).start()
            copy_down(2 * (i - n_hid) + 1).start()

    for i in range(AHEAD):
        start_step(i)

    stage[...] = fold(tok_ref[...].astype(jnp.float32)).astype(jnp.bfloat16)
    own = pltpu.make_async_copy(stage, tokbuf.at[me], tok_recv)
    own.start()
    pl.semaphore_wait(barrier, n_all - 1)

    @pl.loop(1, n_all)
    def _(k):
        to = (me + k) % n_all
        pltpu.make_async_remote_copy(
            src_ref=stage, dst_ref=tokbuf.at[me], send_sem=tok_send, recv_sem=tok_recv,
            device_id=(to // n_dp, to % n_dp), device_id_type=MESH,
        ).start()

    for i in range(early):
        copy_gate(i).wait()
        copy_up(i).wait()
        start_step(i + AHEAD)
    pltpu.make_async_copy(tokbuf, tokbuf, tok_recv).wait()

    def gather_rows(pair):
        halves = []
        for q in range(2):
            parts = [
                unfold(tokbuf[e * n_dp + pair * 2 + q].astype(jnp.float32))
                for e in range(n_exp)
            ]
            halves.append(jnp.concatenate(parts, axis=1))
        both = jnp.concatenate(halves, axis=0).astype(jnp.bfloat16)
        x[pl.ds(pair * 2 * rows, 2 * rows), :] = both

    each(n_dp // 2, gather_rows)

    @pl.loop(0, n_hid)
    def _(i):
        @pl.when(i >= early)
        def _():
            copy_gate(i).wait()
            copy_up(i).wait()
            start_step(i + AHEAD)

        gate = against_features(x[...], wg[i])
        upper = against_features(x[...], wu[i])
        hid[i] = (gate / (1.0 + jnp.exp(-gate)) * upper).astype(jnp.bfloat16)

    @pl.loop(0, n_col)
    def _(i):
        chunk = chunk_at(i)
        copy_down(i).wait()
        pl.when(i % 2 == 1)(lambda: start_step(n_hid + i // 2 + AHEAD))
        h = jnp.concatenate([hid[j] for j in range(n_hid)], axis=1)
        y[...] = jnp.dot(h, wd[i], preferred_element_type=jnp.float32)

        def send(d):
            for p in range(per):
                e_to = chunk * per + p
                to = e_to * n_dp + d
                block = y[pl.ds(d * rows, rows), starts[p]:starts[p] + span]
                sendbuf[to] = fold(block).astype(jnp.bfloat16)

                @pl.when(to != me)
                def _():
                    pltpu.make_async_remote_copy(
                        src_ref=sendbuf.at[to], dst_ref=recvbuf.at[me],
                        send_sem=out_send, recv_sem=out_recv,
                        device_id=(e_to, d), device_id_type=MESH,
                    ).start()

                @pl.when(to == me)
                def _():
                    pltpu.make_async_copy(sendbuf.at[to], recvbuf.at[me], out_recv).start()

        each(n_dp, send)

    ids = ids_ref[...]
    gates = gates_ref[...]
    shares = []
    for e in range(n_exp):
        one = jnp.sum(jnp.where(ids == e, gates, 0.0), axis=1, keepdims=True)
        shares.append(jnp.concatenate([one, one], axis=0))
    pltpu.make_async_copy(recvbuf, recvbuf, out_recv).wait()
    total = jnp.zeros((2 * rows, span // 2), jnp.float32)
    for e in range(n_exp):
        part = jnp.zeros((2 * rows, span // 2), jnp.float32)
        for d in range(n_dp):
            part = part + recvbuf[e * n_dp + d].astype(jnp.float32)
        total = total + part * shares[e]
    wide = unfold(total)
    for p in range(per):
        @pl.when(e_me % per == p)
        def _():
            at = p * cols - starts[p]
            out_ref[...] = wide[:, at:at + cols].astype(out_ref.dtype)

    pltpu.make_async_copy(
        tokbuf.at[pl.ds(0, n_all - 1)], tokbuf.at[pl.ds(0, n_all - 1)], tok_send
    ).wait()
    pltpu.make_async_copy(
        sendbuf.at[pl.ds(0, n_all - 1)], sendbuf.at[pl.ds(0, n_all - 1)], out_send
    ).wait()


def local(n_exp, n_dp, tokens, expert_ids, gate_values, w_gate, w_up, w_down):
    rows, cols = tokens.shape
    _, hidden, width = w_gate.shape
    all_rows = rows * n_dp
    n_all = n_exp * n_dp
    hid_block = min(256, hidden)
    col_block = cols
    while col_block % 128:
        col_block *= 2
    n_hid, n_col = hidden // hid_block, width // col_block
    span = spans(cols, col_block)[1]
    vmem = pl.BlockSpec(memory_space=pltpu.VMEM)
    hbm = pl.BlockSpec(memory_space=pl.ANY)
    bf16, f32 = jnp.bfloat16, jnp.float32
    return pl.pallas_call(
        functools.partial(kernel, n_exp, n_dp, hid_block, col_block),
        out_shape=jax.ShapeDtypeStruct((rows, cols), bf16),
        in_specs=[vmem, vmem, vmem, hbm, hbm, hbm],
        out_specs=vmem,
        scratch_shapes=[
            pltpu.VMEM((n_hid, hid_block, width), bf16),
            pltpu.VMEM((n_hid, hid_block, width), bf16),
            pltpu.VMEM((n_col, hidden, col_block), bf16),
            pltpu.VMEM((2 * rows, cols // 2), bf16),
            pltpu.VMEM((n_all, 2 * rows, cols // 2), bf16),
            pltpu.VMEM((all_rows, width), bf16),
            pltpu.VMEM((n_hid, all_rows, hid_block), bf16),
            pltpu.VMEM((all_rows, col_block), f32),
            pltpu.VMEM((n_all, 2 * rows, span // 2), bf16),
            pltpu.VMEM((n_all, 2 * rows, span // 2), bf16),
            pltpu.SemaphoreType.DMA((n_hid,)),
            pltpu.SemaphoreType.DMA((n_hid,)),
            pltpu.SemaphoreType.DMA((n_col,)),
            pltpu.SemaphoreType.DMA,
            pltpu.SemaphoreType.DMA,
            pltpu.SemaphoreType.DMA,
            pltpu.SemaphoreType.DMA,
        ],
        compiler_params=pltpu.CompilerParams(
            collective_id=0, has_side_effects=True, vmem_limit_bytes=56 * 1024 * 1024
        ),
    )(tokens, expert_ids, gate_values, w_gate[0], w_up[0], w_down[0])


def solution(mesh):
    placed = (
        P("dp", "expert"),
        P("dp", None),
        P("dp", None),
        P("expert", "dp", None),
        P("expert", "dp", None),
        P("expert", "dp", None),
    )
    return jax.shard_map(
        functools.partial(local, mesh.shape["expert"], mesh.shape["dp"]),
        mesh=mesh, in_specs=placed, out_specs=P("dp", "expert"), check_vma=False,
    )
```

```python
import functools

import jax
import jax.numpy as jnp
from jax import lax
from jax.experimental import pallas as pl
from jax.experimental.pallas import tpu as pltpu
from jax.sharding import PartitionSpec as P

MESH = pl.DeviceIdType.MESH
AHEAD = 2
EARLY = 2


def against_features(piece, weight):
    return lax.dot_general(
        piece, weight, (((1,), (1,)), ((), ())), preferred_element_type=jnp.float32
    )


def spans(cols, col_block):
    first = [p * cols // 128 * 128 for p in range(col_block // cols)]
    need = max(p * cols - start + cols for p, start in enumerate(first))
    width = -(-need // 256) * 256
    return [min(start, col_block - width) for start in first], width


def each(count, body):
    if count <= 4:
        for i in range(count):
            body(i)
    else:
        @pl.loop(0, count)
        def _(i):
            body(i)


def fold(block):
    half = block.shape[1] // 2
    return jnp.concatenate([block[:, :half], block[:, half:]], axis=0)


def unfold(block):
    half = block.shape[0] // 2
    return jnp.concatenate([block[:half], block[half:]], axis=1)


def kernel(
    n_exp, n_dp, hid_block, col_block,
    tok_ref, ids_ref, gates_ref, wg_hbm, wu_hbm, wd_hbm, out_ref,
    wg, wu, wd, stage, tokbuf, x, hid, y, sendbuf, recvbuf,
    g_sem, u_sem, d_sem, fwd_send, fwd_recv, tok_send, tok_recv, out_send, out_recv,
):
    n_all = n_exp * n_dp
    rows, cols = tok_ref.shape
    n_hid = wg.shape[0]
    n_col = wd.shape[0]
    per = col_block // cols
    n_pair = n_col // 2
    starts, span = spans(cols, col_block)
    early = min(EARLY, n_hid)
    e_me = lax.axis_index("expert")
    d_me = lax.axis_index("dp")
    me = e_me * n_dp + d_me
    home = e_me // per

    def chunk_at(i):
        i = jnp.int32(i)
        turn = n_col // 2 + (1 - 2 * (i % 2)) * ((i + 1) // 2)
        return (home + turn) % n_col

    def copy_gate(i):
        at = pl.ds(i * hid_block, hid_block)
        return pltpu.make_async_copy(wg_hbm.at[at], wg.at[i], g_sem.at[i])

    def copy_up(i):
        at = pl.ds(i * hid_block, hid_block)
        return pltpu.make_async_copy(wu_hbm.at[at], wu.at[i], u_sem.at[i])

    def copy_down(i):
        start = pl.multiple_of(chunk_at(i) * col_block, 128)
        return pltpu.make_async_copy(
            wd_hbm.at[:, pl.ds(start, col_block)], wd.at[i], d_sem.at[i]
        )

    barrier = pltpu.get_barrier_semaphore()

    @pl.loop(1, n_all)
    def _(k):
        to = (me + k) % n_all
        pl.semaphore_signal(
            barrier, inc=1, device_id=(to // n_dp, to % n_dp), device_id_type=MESH
        )

    def start_hid(i):
        copy_gate(i).start()
        copy_up(i).start()

    def start_step(i):
        if isinstance(i, int):
            if i < n_hid:
                start_hid(i)
            elif i < n_hid + n_pair:
                copy_down(2 * (i - n_hid)).start()
                copy_down(2 * (i - n_hid) + 1).start()
            return
        pl.when(i < n_hid)(lambda: start_hid(i))

        @pl.when((i >= n_hid) & (i < n_hid + n_pair))
        def _():
            copy_down(2 * (i - n_hid)).start()
            copy_down(2 * (i - n_hid) + 1).start()

    for i in range(AHEAD):
        start_step(i)

    stage[...] = fold(tok_ref[...].astype(jnp.float32)).astype(jnp.bfloat16)
    side = e_me % 2
    n_side = n_all // 2
    slot = e_me // 2 * n_dp + d_me
    own = pltpu.make_async_copy(stage, tokbuf.at[side, slot], tok_recv)
    own.start()
    pl.semaphore_wait(barrier, n_all - 1)

    @pl.loop(1, n_side)
    def _(k):
        to = (slot + k) % n_side
        pltpu.make_async_remote_copy(
            src_ref=stage, dst_ref=tokbuf.at[side, slot], send_sem=tok_send,
            recv_sem=tok_recv, device_id=(to // n_dp * 2 + side, to % n_dp),
            device_id_type=MESH,
        ).start()

    def early_step(i):
        copy_gate(i).wait()
        copy_up(i).wait()
        start_step(i + AHEAD)

    early_step(0)
    pltpu.make_async_copy(tokbuf.at[side], tokbuf.at[side], tok_recv).wait()
    forward = pltpu.make_async_remote_copy(
        src_ref=tokbuf.at[side], dst_ref=tokbuf.at[side], send_sem=fwd_send,
        recv_sem=fwd_recv, device_id=(e_me + 1 - 2 * side, d_me), device_id_type=MESH,
    )
    forward.start()
    for i in range(1, early):
        early_step(i)
    pltpu.make_async_copy(tokbuf.at[side], tokbuf.at[side], fwd_recv).wait()

    def gather_rows(pair):
        halves = []
        for q in range(2):
            parts = [
                unfold(tokbuf[e % 2, e // 2 * n_dp + pair * 2 + q].astype(jnp.float32))
                for e in range(n_exp)
            ]
            halves.append(jnp.concatenate(parts, axis=1))
        both = jnp.concatenate(halves, axis=0).astype(jnp.bfloat16)
        x[pl.ds(pair * 2 * rows, 2 * rows), :] = both

    each(n_dp // 2, gather_rows)

    def hid_step(i):
        @pl.when(jnp.int32(i) >= early)
        def _():
            copy_gate(i).wait()
            copy_up(i).wait()
            start_step(i + AHEAD)

        gate = against_features(x[...], wg[i])
        upper = against_features(x[...], wu[i])
        hid[i] = (gate / (1.0 + jnp.exp(-gate)) * upper).astype(jnp.bfloat16)

    each(n_hid, hid_step)

    @pl.loop(0, n_col)
    def _(i):
        chunk = chunk_at(i)
        copy_down(i).wait()
        pl.when(i % 2 == 1)(lambda: start_step(n_hid + i // 2 + AHEAD))
        h = jnp.concatenate([hid[j] for j in range(n_hid)], axis=1)
        y[...] = jnp.dot(h, wd[i], preferred_element_type=jnp.float32)

        def send(d):
            for p in range(per):
                e_to = chunk * per + p
                to = e_to * n_dp + d
                block = y[pl.ds(d * rows, rows), starts[p]:starts[p] + span]
                sendbuf[to] = fold(block).astype(jnp.bfloat16)

                @pl.when(to != me)
                def _():
                    pltpu.make_async_remote_copy(
                        src_ref=sendbuf.at[to], dst_ref=recvbuf.at[me],
                        send_sem=out_send, recv_sem=out_recv,
                        device_id=(e_to, d), device_id_type=MESH,
                    ).start()

                @pl.when(to == me)
                def _():
                    pltpu.make_async_copy(sendbuf.at[to], recvbuf.at[me], out_recv).start()

        each(n_dp, send)

    ids = ids_ref[...]
    gates = gates_ref[...]
    shares = []
    for e in range(n_exp):
        one = jnp.sum(jnp.where(ids == e, gates, 0.0), axis=1, keepdims=True)
        shares.append(jnp.concatenate([one, one], axis=0))
    pltpu.make_async_copy(recvbuf, recvbuf, out_recv).wait()
    total = jnp.zeros((2 * rows, span // 2), jnp.float32)
    for e in range(n_exp):
        part = jnp.zeros((2 * rows, span // 2), jnp.float32)
        for d in range(n_dp):
            part = part + recvbuf[e * n_dp + d].astype(jnp.float32)
        total = total + part * shares[e]
    wide = unfold(total)
    for p in range(per):
        @pl.when(e_me % per == p)
        def _():
            at = p * cols - starts[p]
            out_ref[...] = wide[:, at:at + cols].astype(out_ref.dtype)

    pltpu.make_async_copy(
        tokbuf.at[0, pl.ds(0, n_side - 1)], tokbuf.at[0, pl.ds(0, n_side - 1)], tok_send
    ).wait()
    pltpu.make_async_copy(tokbuf.at[side], tokbuf.at[side], fwd_send).wait()
    pltpu.make_async_copy(
        sendbuf.at[pl.ds(0, n_all - 1)], sendbuf.at[pl.ds(0, n_all - 1)], out_send
    ).wait()


def local(n_exp, n_dp, tokens, expert_ids, gate_values, w_gate, w_up, w_down):
    rows, cols = tokens.shape
    _, hidden, width = w_gate.shape
    all_rows = rows * n_dp
    n_all = n_exp * n_dp
    hid_block = min(256, hidden)
    col_block = cols
    while col_block % 128:
        col_block *= 2
    n_hid, n_col = hidden // hid_block, width // col_block
    span = spans(cols, col_block)[1]
    vmem = pl.BlockSpec(memory_space=pltpu.VMEM)
    hbm = pl.BlockSpec(memory_space=pl.ANY)
    bf16, f32 = jnp.bfloat16, jnp.float32
    return pl.pallas_call(
        functools.partial(kernel, n_exp, n_dp, hid_block, col_block),
        out_shape=jax.ShapeDtypeStruct((rows, cols), bf16),
        in_specs=[vmem, vmem, vmem, hbm, hbm, hbm],
        out_specs=vmem,
        scratch_shapes=[
            pltpu.VMEM((n_hid, hid_block, width), bf16),
            pltpu.VMEM((n_hid, hid_block, width), bf16),
            pltpu.VMEM((n_col, hidden, col_block), bf16),
            pltpu.VMEM((2 * rows, cols // 2), bf16),
            pltpu.VMEM((2, n_all // 2, 2 * rows, cols // 2), bf16),
            pltpu.VMEM((all_rows, width), bf16),
            pltpu.VMEM((n_hid, all_rows, hid_block), bf16),
            pltpu.VMEM((all_rows, col_block), f32),
            pltpu.VMEM((n_all, 2 * rows, span // 2), bf16),
            pltpu.VMEM((n_all, 2 * rows, span // 2), bf16),
            pltpu.SemaphoreType.DMA((n_hid,)),
            pltpu.SemaphoreType.DMA((n_hid,)),
            pltpu.SemaphoreType.DMA((n_col,)),
            pltpu.SemaphoreType.DMA,
            pltpu.SemaphoreType.DMA,
            pltpu.SemaphoreType.DMA,
            pltpu.SemaphoreType.DMA,
            pltpu.SemaphoreType.DMA,
            pltpu.SemaphoreType.DMA,
        ],
        compiler_params=pltpu.CompilerParams(
            collective_id=0, has_side_effects=True, vmem_limit_bytes=56 * 1024 * 1024
        ),
    )(tokens, expert_ids, gate_values, w_gate[0], w_up[0], w_down[0])


def solution(mesh):
    placed = (
        P("dp", "expert"),
        P("dp", None),
        P("dp", None),
        P("expert", "dp", None),
        P("expert", "dp", None),
        P("expert", "dp", None),
    )
    return jax.shard_map(
        functools.partial(local, mesh.shape["expert"], mesh.shape["dp"]),
        mesh=mesh, in_specs=placed, out_specs=P("dp", "expert"), check_vma=False,
    )
```
